32 devices in a mesh: groups: 2 (over x), latent: 16 (over z, y, core).
Axes of the slice: x: 2, y: 2, z: 4, core: 2. Of those that a mesh axis runs over, the one named last changes fastest.
Arguments:
- acts: bfloat16 [4096, 8192], P(('groups', 'latent')), parts along dimension 0, may hold values from -6 to 6
- block_ids: int32 [4096, 2], P(('groups', 'latent')), parts along dimension 0, may hold values from 0 to 15, all different within a row; in each aligned block of 128 rows (0 to 127, 128 to 255, ...) at most 32 rows name the same one
- slot_of: int32 [16], replicated, may hold values from 0 to 15, each once
- enc_tiles: bfloat16 [16, 128, 8192], P('latent'), may hold values from -0.0625 to 0.0625
- dec_tiles: bfloat16 [16, 128, 8192], P('latent'), may hold values from -0.375 to 0.375
- enc_bias: float32 [16, 128], P('latent'), may hold values from -3 to 3
- dec_bias: bfloat16 [8192], replicated, may hold values from -3 to 3
Outputs:
- recon: bfloat16 [4096, 8192], P(('groups', 'latent')), parts along dimension 0
- grad_enc: bfloat16 [32, 128, 8192], P(('groups', 'latent')), parts along dimension 0
- grad_dec: bfloat16 [32, 128, 8192], P(('groups', 'latent')), parts along dimension 0
- grad_bias: float32 [32, 128], P(('groups', 'latent')), parts along dimension 0
The draws below stay inside these ranges and needn't reach their ends.
There are 2 independent parts, one for each index of `groups`. The reference program is written for one: setup_inputs(seed, part) draws one part's arguments, and reference() takes and returns one part's arrays. A program takes and returns all parts, laid end to end along the dimension named above; an argument that names none is the same for every part. Nothing has to cross between parts.
Inputs may be any that keep to these rules, and one draw needn't show every extreme that they name: `block_ids`: each row names 2 different blocks. In each aligned block of 128 rows (the rows of one device), no latent block is named by more than 32 rows, and some latent block is named by exactly 32 rows. `slot_of`: A permutation: each slot holds one block.
All inputs are finite; a program needn't handle non-finite values.
Results may differ from the reference program's by a relative error of at most 0.0054.
Values may be sent and summed in bfloat16 or wider, within the bound.
A program may use at most 128 MiB of HBM per device.

```python
import math
import jax
import jax.numpy as jnp
import numpy as np
from jax import lax

D = 8192
LAT = 128
TOPB = 2
TOK_DEV = 128
NBLK = 16
TOKENS = 2048
CAP = 32
N_LATENT = 16


def steps_of(key, shape, cuts, least, top_value):
    gain = 1.0
    for dim, shards_of in cuts:
        heights = jax.random.uniform(jax.random.fold_in(jax.random.fold_in(key, 6), dim), (shards_of,), jnp.float32, least / len(cuts), top_value / len(cuts))
        gain = gain * jnp.repeat(jnp.exp(heights), shape[dim] // shards_of).reshape((-1,) + (1,) * (len(shape) - 1 - dim))
    return gain


def deal_out(stream_key, own, number, rows, count, top, bound, skew):
    order = jax.random.permutation(stream_key, count)
    crowded, ordinary = portions_of(count, rows * top, bound, skew, True), portions_of(count, rows * top, bound, skew, False)
    places = jnp.arange(count)

    def named(lengths, rotation):
        used = int((lengths > 0).sum())
        fixed = max(1, used // 4)
        moved = fixed + (places - fixed + rotation * (used - fixed)) % max(1, count - fixed)
        return jnp.zeros((count,), jnp.int32).at[order[jnp.where(places < fixed, places, moved)]].set(jnp.asarray(lengths, jnp.int32))

    lengths = jnp.where(number % 4 == 0, named(crowded, number // 4), named(ordinary, number - number // 4 - 1))
    mixed = jax.random.permutation(jax.random.fold_in(own, 3), count)
    source_of, receiver = mixed[0:count // 2 * 2:2], mixed[1:count // 2 * 2:2]
    room = jnp.minimum(lengths[source_of] - 1, bound - lengths[receiver]) // 2
    room = jnp.where((source_of == order[0]) | (receiver == order[0]) | (lengths[receiver] == 0), 0, jnp.maximum(room, 0))
    moved = jax.random.randint(jax.random.fold_in(own, 4), (count // 2,), 0, 1 << 20) % (room + 1)
    lengths = lengths.at[source_of].add(-moved).at[receiver].add(moved)
    members = jnp.searchsorted(jnp.cumsum(lengths), jnp.arange(rows * top), side="right").astype(jnp.int32)
    table = members.reshape(top, rows).T
    table = table[jax.random.permutation(jax.random.fold_in(own, 1), rows)]
    rotation = jax.random.randint(jax.random.fold_in(own, 2), (rows, 1), 0, top)
    return jnp.take_along_axis(table, (jnp.arange(top)[None, :] + rotation) % top, axis=1)


def portions_of(count, total, most, skew, full):
    weights = [(1 << 20) // math.isqrt(rank ** skew) + 1 for rank in range(1, count + 1)]
    largest = most if full else min(most, max(-(-total // count), total * weights[0] // sum(weights)))
    least = 1 if total - largest >= count - 1 else 0
    counts, surplus = [largest] + [least] * (count - 1), total - largest - least * (count - 1)
    while surplus > 0:
        candidates = [i for i in range(1, count) if counts[i] < largest] or [i for i in range(1, count) if counts[i] < most]
        mass, budget = sum([weights[i] for i in candidates]), surplus
        for i in candidates:
            addition = min(most - counts[i], max(1, budget * weights[i] // mass), surplus)
            counts[i] = counts[i] + addition
            surplus = surplus - addition
    return np.array(counts)


def noise(own_key, shape, scale, most, split=(), kind=jnp.bfloat16):
    result = jax.random.normal(own_key, shape, jnp.float32) * scale
    if len(split) > 0:
        result = steps_of(own_key, shape, split, -0.22, 0.18) * result
    return jnp.clip(result, min=-most, max=most).astype(kind)


def setup_inputs(seed: int = 0, part: int = 0) -> dict:
    seeds = jax.random.split(jax.random.key(seed), 8)
    part_splits = jax.random.split(jax.random.fold_in(seeds[7], part), 8)
    acts = noise(part_splits[0], (TOKENS, D), 1.0, 6.0, ((0, 16),))
    block_ids_keys = jax.random.split(jax.random.fold_in(part_splits[1], 1), TOKENS // TOK_DEV)
    block_ids_turns = jax.random.permutation(jax.random.fold_in(part_splits[1], 3), TOKENS // TOK_DEV)
    block_ids = jax.vmap(lambda own, number: deal_out(jax.random.fold_in(part_splits[1], 2), own, number, TOK_DEV, NBLK, TOPB, CAP, 2))(block_ids_keys, block_ids_turns).reshape((TOKENS, TOPB))
    slot_of = jax.random.permutation(seeds[2], NBLK).astype(jnp.int32)
    enc_tiles = noise(seeds[3], (NBLK, LAT, D), D ** -0.5, 0.0625, ((0, 16),))
    dec_tiles = noise(seeds[4], (NBLK, LAT, D), (LAT * TOPB) ** -0.5, 0.375, ((0, 16),))
    enc_bias = noise(seeds[5], (NBLK, LAT), 0.5, 3.0, ((0, 16),), jnp.float32)
    dec_bias = noise(seeds[6], (D,), 0.5, 3.0)
    return dict(acts=acts, block_ids=block_ids, slot_of=slot_of, enc_tiles=enc_tiles, dec_tiles=dec_tiles, enc_bias=enc_bias, dec_bias=dec_bias)


def silu_slope(value):
    sig = jax.nn.sigmoid(value)
    return sig * (1.0 + value * (1.0 - sig))


def reference(acts, block_ids, slot_of, enc_tiles, dec_tiles, enc_bias, dec_bias):
    tokens = acts.shape[0]
    topb = block_ids.shape[1]
    nblk = slot_of.shape[0]
    cap_all = N_LATENT * CAP
    flat = block_ids.reshape(-1)
    pairs = flat.shape[0]
    number = jnp.arange(nblk, dtype=jnp.int32)
    block_of_slot = jnp.sum(jnp.where(slot_of[None, :] == number[:, None], number[None, :], 0), axis=1).astype(jnp.int32)

    def select(slot):
        block = block_of_slot[slot]
        marked = flat == block
        rank = jnp.cumsum(marked.astype(jnp.int32)) - 1
        target = jnp.where(marked, rank, cap_all).astype(jnp.int32)
        index = jnp.zeros((cap_all + 1,), jnp.int32).at[target].set(jnp.arange(pairs, dtype=jnp.int32))[:cap_all]
        valid = jnp.arange(cap_all, dtype=jnp.int32) < jnp.sum(marked.astype(jnp.int32))
        return index // topb, valid

    row_of, valid_all = lax.map(select, number)

    def forward_tile(slot):
        rows_idx = row_of[slot]
        valid = valid_all[slot]
        rows = jnp.where(valid[:, None], acts[rows_idx], jnp.zeros((), jnp.bfloat16))
        tile_enc = enc_tiles[slot]
        pre = jnp.dot(rows, tile_enc.T, preferred_element_type=jnp.float32)
        pre = pre - jnp.dot(dec_bias, tile_enc.T, preferred_element_type=jnp.float32)[None, :] + enc_bias[slot][None, :]
        act = jax.nn.silu(pre).astype(jnp.bfloat16)
        return rows, pre, act, valid, rows_idx

    def accumulate(total, slot):
        rows, pre, act, valid, rows_idx = forward_tile(slot)
        part = jnp.dot(act, dec_tiles[slot], preferred_element_type=jnp.float32).astype(jnp.bfloat16)
        part = jnp.where(valid[:, None], part.astype(jnp.float32), 0.0)
        return total.at[rows_idx].add(part), None

    total, unused = lax.scan(accumulate, jnp.zeros((tokens, acts.shape[1]), jnp.float32), number)
    recon_f = total + dec_bias.astype(jnp.float32)[None, :]
    recon = recon_f.astype(jnp.bfloat16)
    err = (recon_f - acts.astype(jnp.float32)).astype(jnp.bfloat16)

    def backward_tile(slot):
        rows, pre, act, valid, rows_idx = forward_tile(slot)
        errors = jnp.where(valid[:, None], err[rows_idx], jnp.zeros((), jnp.bfloat16))
        tile_dec = dec_tiles[slot]
        slope = jnp.dot(errors, tile_dec.T, preferred_element_type=jnp.float32) * silu_slope(pre)
        slope_b = slope.astype(jnp.bfloat16)
        bias_grad = jnp.sum(slope, axis=0)
        dec_grad = jnp.dot(act.T, errors, preferred_element_type=jnp.float32).astype(jnp.bfloat16)
        enc_grad = jnp.dot(slope_b.T, rows, preferred_element_type=jnp.float32)
        enc_grad = (enc_grad - bias_grad[:, None] * dec_bias.astype(jnp.float32)[None, :]).astype(jnp.bfloat16)
        return enc_grad, dec_grad, bias_grad

    grad_enc, grad_dec, grad_bias = lax.map(backward_tile, number)
    return recon, grad_enc, grad_dec, grad_bias
```

```python
import functools

import jax
import jax.numpy as jnp
from jax import lax
from jax.experimental import pallas as pl
from jax.experimental.pallas import tpu as pltpu
from jax.sharding import PartitionSpec as P

BF = jnp.bfloat16
F32 = jnp.float32
NT = (((1,), (1,)), ((), ()))
MESH = pl.DeviceIdType.MESH
SX, SE, SF, ST, SR, SGD, SGE, SGB = range(8)


def place_of(index, nz):
    return (index % 2) * (2 * nz) + ((index // 2) % 2) * nz + index // 4


def device_of(place, nz):
    return (place % nz) * 4 + ((place // nz) % 2) * 2 + place // (2 * nz)


def step_kernel(
    n,
    acts,
    enc,
    dec,
    tgt,
    db_ref,
    bias_ref,
    recon_out,
    genc_out,
    gdec_out,
    gb_out,
    X,
    E,
    F,
    TR,
    TC,
    PP,
    R1,
    R2,
    R3,
    ACT,
    ACTT,
    ERR,
    RO,
    GD,
    GE,
    PRE,
    GB,
    GT,
    send,
    recv,
    ar_send,
    ar_recv,
    local,
):
    nz = n // 4
    rows = acts.shape[0]
    cols = acts.shape[1] // n
    lat = enc.shape[0]
    me = lax.axis_index("latent")
    c = me % 2
    y = (me // 2) % 2
    z = me // 4
    mine = place_of(me, nz)

    def far(off):
        place = (mine + off) % n
        return place, device_of(place, nz)

    def remote(src, dst, ssem, rsem, dev):
        return pltpu.make_async_remote_copy(
            src_ref=src, dst_ref=dst, send_sem=ssem, recv_sem=rsem,
            device_id={"latent": dev}, device_id_type=MESH,
        )

    def colpiece(place):
        return pl.ds(pl.multiple_of(place * cols, cols), cols)

    def rowpiece(place, size=rows):
        return pl.ds(pl.multiple_of(place * size, size), size)

    def lanepiece(place):
        return pl.ds(pl.multiple_of(place * rows, rows), rows)

    def each(fn):
        def go(off, carry):
            fn(off)
            return carry

        lax.fori_loop(1, n, go, 0)

    barrier = pltpu.get_barrier_semaphore()

    def greet(off):
        pl.semaphore_signal(barrier, inc=1, device_id={"latent": far(off)[1]}, device_id_type=MESH)

    each(greet)
    pl.semaphore_wait(barrier, n - 1)

    def inbound(kind, src, dst):
        def make(off):
            place, dev = far(off)
            return remote(src.at[:, colpiece(place)], dst.at[rowpiece(mine)],
                          send.at[kind, off], recv.at[kind, off], dev)

        return make

    def tcopy(off):
        place, dev = far(off)
        return remote(tgt, TR.at[:, lanepiece(mine)], send.at[ST, off], recv.at[ST, off], dev)

    xcopy = inbound(SX, acts, X)
    ecopy = inbound(SE, enc, E)
    fcopy = inbound(SF, dec, F)
    each(lambda off: tcopy(off).start())
    each(lambda off: xcopy(off).start())
    each(lambda off: ecopy(off).start())
    own = [
        pltpu.make_async_copy(acts.at[:, colpiece(mine)], X.at[rowpiece(mine)], local.at[0]),
        pltpu.make_async_copy(enc.at[:, colpiece(mine)], E.at[rowpiece(mine)], local.at[1]),
        pltpu.make_async_copy(dec.at[:, colpiece(mine)], F.at[rowpiece(mine)], local.at[2]),
        pltpu.make_async_copy(tgt, TR.at[:, lanepiece(mine)], local.at[3]),
    ]
    for copy in own:
        copy.start()
    for copy in own:
        copy.wait()
    each(lambda off: tcopy(off).wait())
    each(lambda off: xcopy(off).wait_send())
    each(lambda off: ecopy(off).wait_send())
    each(lambda off: fcopy(off).start())

    def columns(p, carry):
        TC[rowpiece(p), :] = jnp.transpose(TR[:, lanepiece(p)])
        return carry

    lax.fori_loop(0, n, columns, 0)
    each(lambda off: xcopy(off).wait_recv())
    each(lambda off: ecopy(off).wait_recv())

    db = db_ref[...]
    db_row = db[0:1, :]
    corr = bias_ref[...] - lax.dot_general(db.astype(BF), E[...], NT, preferred_element_type=F32)
    corr_row = corr[0:1, :]
    block = 2 * rows

    def pick(r, full):
        for j in range(2):
            t = TC[r, j : j + 1]
            total = jnp.zeros((block, lat), F32)
            for s in range(n):
                total = jnp.where(t == float(s), full[:, s * lat : (s + 1) * lat], total)
            PP[r, j * lat : (j + 1) * lat] = total

    def encode(i, carry):
        r = rowpiece(i, block)
        full = lax.dot_general(X[r, :], E[...], NT, preferred_element_type=F32) + corr_row
        pick(r, full)
        return carry

    lax.fori_loop(0, n // 2, encode, 0)

    def reduce_own(phase, after_first, after_third):
        peer_c, peer_y = z * 4 + y * 2 + (1 - c), z * 4 + (1 - y) * 2 + c
        half, quarter = 2 * nz * rows, nz * rows
        one = remote(PP.at[rowpiece(1 - c, half)], R1.at[phase], ar_send.at[phase, 0], ar_recv.at[phase, 0], peer_c)
        one.start()
        after_first()
        one.wait()
        mine_half = c * 2

        def add(base_rows, buffer, pieces):
            def go(i, carry):
                r = rowpiece(base_rows + i)
                PP[r, :] = PP[r, :] + buffer[phase, rowpiece(i), :]
                return carry

            lax.fori_loop(0, pieces, go, 0)

        add(c * 2 * nz, R1, 2 * nz)
        two = remote(PP.at[rowpiece(mine_half + 1 - y, quarter)], R2.at[phase], ar_send.at[phase, 1], ar_recv.at[phase, 1], peer_y)
        two.start()
        two.wait()
        add((mine_half + y) * nz, R2, nz)
        third = []
        for dz in range(1, nz):
            oz = (z + dz) % nz
            copy = remote(PP.at[rowpiece((mine_half + y) * nz + oz)], R3.at[phase, dz - 1],
                          ar_send.at[phase, 1 + dz], ar_recv.at[phase, 1 + dz], oz * 4 + y * 2 + c)
            copy.start()
            third.append(copy)
        after_third()
        for copy in third:
            copy.wait()
        total = PP[rowpiece(mine), :]
        for dz in range(1, nz):
            total = total + R3[phase, dz - 1]
        return total

    def spread(phase, between=lambda: None):
        peer_c, peer_y = z * 4 + y * 2 + (1 - c), z * 4 + (1 - y) * 2 + c
        half, quarter = 2 * nz * rows, nz * rows
        base = 1 + nz
        piece = ACT.at[phase, rowpiece(mine)]
        copies = []
        for dz in range(1, nz):
            oz = (z + dz) % nz
            copy = remote(piece, piece, ar_send.at[phase, base + dz], ar_recv.at[phase, base + dz], oz * 4 + y * 2 + c)
            copy.start()
            copies.append(copy)
        between()
        for copy in copies:
            copy.wait()
        piece = ACT.at[phase, rowpiece(c * 2 + y, quarter)]
        copy = remote(piece, piece, ar_send.at[phase, base + nz], ar_recv.at[phase, base + nz], peer_y)
        copy.start()
        copy.wait()
        piece = ACT.at[phase, rowpiece(c, half)]
        copy = remote(piece, piece, ar_send.at[phase, base + nz + 1], ar_recv.at[phase, base + nz + 1], peer_c)
        copy.start()
        copy.wait()

    pre = reduce_own(0, lambda: None, lambda: None)
    PRE[...] = pre
    ACT[0, rowpiece(mine), :] = (pre / (1.0 + jnp.exp(-pre))).astype(BF)
    spread(0)

    each(lambda off: fcopy(off).wait())

    def decode(i, carry):
        r = rowpiece(i, block)
        act = ACT[0, r, :]
        t0, t1 = TC[r, 0:1], TC[r, 1:2]
        a0, a1 = act[:, :lat].astype(F32), act[:, lat:].astype(F32)
        wide = jnp.concatenate(
            [jnp.where(t0 == float(s), a0, jnp.where(t1 == float(s), a1, 0.0)).astype(BF) for s in range(n)],
            axis=1,
        )
        recon_f = jnp.dot(wide, F[...], preferred_element_type=F32) + db_row
        RO[r, :] = recon_f.astype(BF)
        err = (recon_f - X[r, :].astype(F32)).astype(BF)
        ERR[r, :] = err
        pick(r, lax.dot_general(err, F[...], NT, preferred_element_type=F32))
        return carry

    lax.fori_loop(0, n // 2, decode, 0)

    def outbound(kind, src, dst):
        def make(off):
            place, dev = far(off)
            return remote(src.at[rowpiece(place)], dst.at[:, colpiece(mine)],
                          send.at[kind, off], recv.at[kind, off], dev)

        return make

    def keep(src, dst, slot):
        return pltpu.make_async_copy(src.at[rowpiece(mine)], dst.at[:, colpiece(mine)], local.at[slot])

    rcopy = outbound(SR, RO, recon_out)
    dcopy = outbound(SGD, GD, gdec_out)
    gcopy = outbound(SGE, GE, genc_out)
    keeps = [keep(RO, recon_out, 4), keep(GD, gdec_out, 5), keep(GE, genc_out, 6)]

    def turn(phase):
        def go(p, carry):
            ACTT[:, lanepiece(p)] = jnp.transpose(ACT[phase, rowpiece(p), :].astype(F32)).astype(BF)
            return carry

        lax.fori_loop(0, n, go, 0)

    def grad_tile(s, other):
        sf = s.astype(F32)
        t0, t1 = TR[0:1, :], TR[1:2, :]
        picked = jnp.where(
            t0 == sf,
            ACTT[:lat, :].astype(F32),
            jnp.where(t1 == sf, ACTT[lat:, :].astype(F32), 0.0),
        ).astype(BF)
        return jnp.dot(picked, other[...], preferred_element_type=F32)

    def decoder_grad():
        turn(0)

        def go(s, carry):
            GD[rowpiece(s), :] = grad_tile(s, ERR).astype(BF)
            return carry

        lax.fori_loop(0, n, go, 0)

    def first():
        each(lambda off: rcopy(off).start())
        keeps[0].start()
        decoder_grad()

    def third():
        each(lambda off: dcopy(off).start())
        keeps[1].start()

    slope = reduce_own(1, first, third)
    value = PRE[...]
    sig = 1.0 / (1.0 + jnp.exp(-value))
    dpre = slope * (sig * (1.0 + value * (1.0 - sig)))
    ACT[1, rowpiece(mine), :] = dpre.astype(BF)
    t0, t1 = TC[rowpiece(mine), 0:1], TC[rowpiece(mine), 1:2]
    for s in range(n):
        share = jnp.where(t0 == float(s), dpre[:, :lat], 0.0) + jnp.where(t1 == float(s), dpre[:, lat:], 0.0)
        GT[s : s + 1, :] = jnp.sum(share, axis=0, keepdims=True)

    def bcopy(off):
        place, dev = far(off)
        return remote(GT, GB.at[mine], send.at[SGB, off], recv.at[SGB, off], dev)

    each(lambda off: bcopy(off).start())
    spread(1)
    GB[mine] = GT[...]
    each(lambda off: bcopy(off).wait())
    grad_b = jnp.sum(GB[...], axis=0)
    grad_cols = jnp.transpose(grad_b)
    gb_out[...] = grad_b
    turn(1)

    def encoder_grad(s, carry):
        lane = lax.broadcasted_iota(jnp.int32, (lat, n), 1)
        col = jnp.sum(jnp.where(lane == s, grad_cols, 0.0), axis=1, keepdims=True)
        GE[rowpiece(s), :] = (grad_tile(s, X) - col * db_row).astype(BF)
        return carry

    lax.fori_loop(0, n, encoder_grad, 0)
    each(lambda off: gcopy(off).start())
    keeps[2].start()
    each(lambda off: rcopy(off).wait())
    each(lambda off: dcopy(off).wait())
    each(lambda off: gcopy(off).wait())
    for copy in keeps:
        copy.wait()


def sliced_body(acts, block_ids, slot_of, enc_tiles, dec_tiles, enc_bias, dec_bias):
    n = lax.axis_size("latent")
    nz = n // 4
    rows, width = acts.shape
    lat = enc_tiles.shape[1]
    cols = width // n
    me = lax.axis_index("latent")
    mine = place_of(me, nz)
    picked = block_ids[:, :, None] == jnp.arange(n, dtype=jnp.int32)[None, None, :]
    target = jnp.sum(jnp.where(picked, place_of(slot_of, nz)[None, None, :], 0), axis=2)
    tgt = jnp.zeros((8, rows), F32).at[:2].set(target.T.astype(F32))
    db = lax.dynamic_slice(dec_bias, (mine * cols,), (cols,)).astype(F32)
    db = jnp.broadcast_to(db[None, :], (8, cols))
    here = jnp.arange(n, dtype=jnp.int32) == mine
    bias = jnp.where(here[:, None], enc_bias[0][None, :], 0.0).reshape(1, n * lat)
    bias = jnp.broadcast_to(bias, (8, n * lat))
    hbm = pl.BlockSpec(memory_space=pl.ANY)
    vmem = pl.BlockSpec(memory_space=pltpu.VMEM)
    all_rows = n * rows
    sem = pltpu.SemaphoreType.DMA
    recon, genc, gdec, gb = pl.pallas_call(
        functools.partial(step_kernel, n),
        out_shape=(
            jax.ShapeDtypeStruct((rows, width), BF),
            jax.ShapeDtypeStruct((lat, width), BF),
            jax.ShapeDtypeStruct((lat, width), BF),
            jax.ShapeDtypeStruct((n, lat), F32),
        ),
        in_specs=[hbm, hbm, hbm, vmem, vmem, vmem],
        out_specs=(hbm, hbm, hbm, vmem),
        scratch_shapes=[
            pltpu.VMEM((all_rows, cols), BF),
            pltpu.VMEM((n * lat, cols), BF),
            pltpu.VMEM((n * lat, cols), BF),
            pltpu.VMEM((8, all_rows), F32),
            pltpu.VMEM((all_rows, 8), F32),
            pltpu.VMEM((all_rows, 2 * lat), F32),
            pltpu.VMEM((2, all_rows // 2, 2 * lat), F32),
            pltpu.VMEM((2, all_rows // 4, 2 * lat), F32),
            pltpu.VMEM((2, nz - 1, rows, 2 * lat), F32),
            pltpu.VMEM((2, all_rows, 2 * lat), BF),
            pltpu.VMEM((2 * lat, all_rows), BF),
            pltpu.VMEM((all_rows, cols), BF),
            pltpu.VMEM((all_rows, cols), BF),
            pltpu.VMEM((n * lat, cols), BF),
            pltpu.VMEM((n * lat, cols), BF),
            pltpu.VMEM((rows, 2 * lat), F32),
            pltpu.VMEM((n, n, lat), F32),
            pltpu.VMEM((n, lat), F32),
            sem((8, n)),
            sem((8, n)),
            sem((2, 4 + 2 * nz)),
            sem((2, 4 + 2 * nz)),
            sem((8,)),
        ],
        compiler_params=pltpu.CompilerParams(
            collective_id=0, has_side_effects=True, vmem_limit_bytes=56 * 1024 * 1024
        ),
        cost_estimate=pl.CostEstimate(
            flops=5 * 2 * all_rows * n * lat * cols, bytes_accessed=24 << 20, transcendentals=0
        ),
    )(acts, enc_tiles[0], dec_tiles[0], tgt, db, bias)
    bias_grad = jnp.sum(jnp.where(here[:, None], gb, 0.0), axis=0)
    return (recon, genc[None], gdec[None], bias_grad[None])


def silu_slope(value):
    sig = jax.nn.sigmoid(value)
    return sig * (1.0 + value * (1.0 - sig))


def encode_rows(rows, tile_enc, tile_dec, bias_row, dec_bias):
    pre = jnp.dot(rows, tile_enc.T, preferred_element_type=jnp.float32)
    pre = (
        pre
        - jnp.dot(dec_bias, tile_enc.T, preferred_element_type=jnp.float32)[None, :]
        + bias_row[None, :]
    )
    act = jax.nn.silu(pre).astype(jnp.bfloat16)
    part = jnp.dot(act, tile_dec, preferred_element_type=jnp.float32).astype(jnp.bfloat16)
    return (pre, act, part)


def routed_body(acts, block_ids, slot_of, enc_tiles, dec_tiles, enc_bias, dec_bias):
    devices = lax.axis_size("latent")
    tok_rows, topb = block_ids.shape
    width = acts.shape[1]
    nblk = slot_of.shape[0]
    capacity = 2 * tok_rows * topb // devices
    flat = block_ids.reshape(-1)
    pairs = flat.shape[0]
    picked = flat[:, None] == jnp.arange(nblk, dtype=jnp.int32)[None, :]
    target = jnp.sum(jnp.where(picked, slot_of[None, :], 0), axis=1)
    marks = (target[:, None] == jnp.arange(devices, dtype=jnp.int32)[None, :]).astype(jnp.int32)
    rank = jnp.sum((jnp.cumsum(marks, axis=0) - 1) * marks, axis=1)
    position = target * capacity + rank
    source = jnp.arange(pairs, dtype=jnp.int32) // topb
    outgoing = jnp.zeros((devices * capacity, width), jnp.bfloat16).at[position].set(acts[source])
    outgoing = outgoing.reshape(devices, capacity, width)
    tile_enc = enc_tiles[0]
    tile_dec = dec_tiles[0]
    bias_row = enc_bias[0]
    arrived = lax.all_to_all(outgoing, "latent", split_axis=0, concat_axis=0, tiled=True).reshape(
        devices * capacity, width
    )
    pre, act, part = encode_rows(arrived, tile_enc, tile_dec, bias_row, dec_bias)
    returned = lax.all_to_all(
        part.reshape(devices, capacity, width), "latent", split_axis=0, concat_axis=0, tiled=True
    )
    returned = returned.reshape(devices * capacity, width)
    gathered = returned[position].astype(jnp.float32).reshape(tok_rows, topb, width)
    recon_f = jnp.sum(gathered, axis=1) + dec_bias.astype(jnp.float32)[None, :]
    recon = recon_f.astype(jnp.bfloat16)
    err = (recon_f - acts.astype(jnp.float32)).astype(jnp.bfloat16)
    err_out = jnp.zeros((devices * capacity, width), jnp.bfloat16).at[position].set(err[source])
    errors = lax.all_to_all(
        err_out.reshape(devices, capacity, width), "latent", split_axis=0, concat_axis=0, tiled=True
    )
    errors = errors.reshape(devices * capacity, width)
    slope = jnp.dot(errors, tile_dec.T, preferred_element_type=jnp.float32) * silu_slope(pre)
    slope_b = slope.astype(jnp.bfloat16)
    bias_grad = jnp.sum(slope, axis=0)
    dec_grad = jnp.dot(act.T, errors, preferred_element_type=jnp.float32).astype(jnp.bfloat16)
    enc_grad = jnp.dot(slope_b.T, arrived, preferred_element_type=jnp.float32)
    enc_grad = (enc_grad - bias_grad[:, None] * dec_bias.astype(jnp.float32)[None, :]).astype(
        jnp.bfloat16
    )
    return (recon, enc_grad[None], dec_grad[None], bias_grad[None])


def body(acts, block_ids, slot_of, enc_tiles, dec_tiles, enc_bias, dec_bias):
    devices = lax.axis_size("latent")
    small = devices == 16 and block_ids.shape[1] == 2 and slot_of.shape[0] == devices
    chosen = sliced_body if small else routed_body
    return chosen(acts, block_ids, slot_of, enc_tiles, dec_tiles, enc_bias, dec_bias)


def solution(mesh):
    in_specs = (
        P(("groups", "latent"), None),
        P(("groups", "latent"), None),
        P(),
        P("latent", None, None),
        P("latent", None, None),
        P("latent", None),
        P(),
    )
    out_specs = (
        P(("groups", "latent"), None),
        P(("groups", "latent"), None, None),
        P(("groups", "latent"), None, None),
        P(("groups", "latent"), None),
    )
    return jax.shard_map(body, mesh=mesh, in_specs=in_specs, out_specs=out_specs, check_vma=False)
```

```python
import functools

import jax
import jax.numpy as jnp
from jax import lax
from jax.experimental import pallas as pl
from jax.experimental.pallas import tpu as pltpu
from jax.sharding import PartitionSpec as P

BF = jnp.bfloat16
F32 = jnp.float32
NT = (((1,), (1,)), ((), ()))
MESH = pl.DeviceIdType.MESH
SX, SE, SF, ST, SR, SGD, SGE, SGB, SEX, SFX = range(10)


def place_of(index, nz):
    return (index % 2) * (2 * nz) + ((index // 2) % 2) * nz + index // 4


def device_of(place, nz):
    return (place % nz) * 4 + ((place // nz) % 2) * 2 + place // (2 * nz)


def step_kernel(
    n,
    acts,
    enc,
    dec,
    tgt,
    db_ref,
    bias_ref,
    recon_out,
    genc_out,
    gdec_out,
    gb_out,
    X,
    E,
    F,
    TR,
    TC,
    PP,
    R1,
    R2,
    R3,
    ACT,
    ACTT,
    ERR,
    RO,
    GD,
    GE,
    PRE,
    GB,
    GT,
    send,
    recv,
    ar_send,
    ar_recv,
    local,
):
    nz = n // 4
    rows = acts.shape[0]
    cols = acts.shape[1] // n
    lat = enc.shape[0]
    me = lax.axis_index("latent")
    c = me % 2
    y = (me // 2) % 2
    z = me // 4
    mine = place_of(me, nz)
    g = lax.axis_index("groups")
    share = lat // 2

    def far(off):
        place = (mine + off) % n
        return place, device_of(place, nz)

    def remote(src, dst, ssem, rsem, dev):
        return pltpu.make_async_remote_copy(
            src_ref=src, dst_ref=dst, send_sem=ssem, recv_sem=rsem,
            device_id={"latent": dev}, device_id_type=MESH,
        )

    def colpiece(place):
        return pl.ds(pl.multiple_of(place * cols, cols), cols)

    def rowpiece(place, size=rows):
        return pl.ds(pl.multiple_of(place * size, size), size)

    def lanepiece(place):
        return pl.ds(pl.multiple_of(place * rows, rows), rows)

    def each(fn):
        def go(off, carry):
            fn(off)
            return carry

        lax.fori_loop(1, n, go, 0)

    barrier = pltpu.get_barrier_semaphore()

    def greet(off):
        pl.semaphore_signal(barrier, inc=1, device_id={"latent": far(off)[1]}, device_id_type=MESH)

    each(greet)
    twin = {"groups": 1 - g, "latent": me}
    pl.semaphore_signal(barrier, inc=1, device_id=twin, device_id_type=MESH)
    pl.semaphore_wait(barrier, n)

    def inbound(kind, src, dst):
        def make(off):
            place, dev = far(off)
            return remote(src.at[:, colpiece(place)], dst.at[rowpiece(mine)],
                          send.at[kind, off], recv.at[kind, off], dev)

        return make

    def tile_rows(place):
        return pl.ds(pl.multiple_of(place * lat + g * share, share), share)

    def tile_inbound(kind, src, dst):
        def make(off):
            place, dev = far(off)
            return remote(src.at[pl.ds(pl.multiple_of(g * share, share), share), colpiece(place)],
                          dst.at[tile_rows(mine)], send.at[kind, off], recv.at[kind, off], dev)

        return make

    def tile_forward(kind, dst):
        def make(off):
            piece = dst.at[tile_rows((mine - off + n) % n)]
            return pltpu.make_async_remote_copy(
                src_ref=piece, dst_ref=piece, send_sem=send.at[kind, off], recv_sem=recv.at[kind, off],
                device_id=twin, device_id_type=MESH,
            )

        return make

    def tcopy(off):
        place, dev = far(off)
        return remote(tgt, TR.at[:, lanepiece(mine)], send.at[ST, off], recv.at[ST, off], dev)

    xcopy = inbound(SX, acts, X)
    ecopy = tile_inbound(SE, enc, E)
    fcopy = tile_inbound(SF, dec, F)
    ecross = tile_forward(SEX, E)
    fcross = tile_forward(SFX, F)
    each(lambda off: tcopy(off).start())
    each(lambda off: ecopy(off).start())
    each(lambda off: xcopy(off).start())
    own = [
        pltpu.make_async_copy(acts.at[:, colpiece(mine)], X.at[rowpiece(mine)], local.at[0]),
        pltpu.make_async_copy(enc.at[:, colpiece(mine)], E.at[rowpiece(mine)], local.at[1]),
        pltpu.make_async_copy(dec.at[:, colpiece(mine)], F.at[rowpiece(mine)], local.at[2]),
        pltpu.make_async_copy(tgt, TR.at[:, lanepiece(mine)], local.at[3]),
    ]
    for copy in own:
        copy.start()
    for copy in own:
        copy.wait()
    each(lambda off: tcopy(off).wait())

    def pass_on(copy, cross):
        def go(off):
            copy(off).wait_recv()
            cross(off).start()

        return go

    def columns(p, carry):
        TC[rowpiece(p), :] = jnp.transpose(TR[:, lanepiece(p)])
        return carry

    lax.fori_loop(0, n, columns, 0)
    each(pass_on(ecopy, ecross))
    each(lambda off: ecross(off).wait())

    db = db_ref[...]
    db_row = db[0:1, :]
    corr = bias_ref[...] - lax.dot_general(db.astype(BF), E[...], NT, preferred_element_type=F32)
    corr_row = corr[0:1, :]
    block = 2 * rows

    def pick(r, full):
        for j in range(2):
            t = TC[r, j : j + 1]
            total = jnp.zeros((block, lat), F32)
            for s in range(n):
                total = jnp.where(t == float(s), full[:, s * lat : (s + 1) * lat], total)
            PP[r, j * lat : (j + 1) * lat] = total

    def encode(i, carry):
        b = (mine // 2 - i + n) % (n // 2)

        @pl.when(i == n // 2 - 2)
        def _():
            each(lambda off: ecopy(off).wait_send())
            each(lambda off: xcopy(off).wait_send())
            each(lambda off: fcopy(off).start())

        for q in range(2):
            off = (mine - 2 * b - q + n) % n

            @pl.when(off != 0)
            def _():
                xcopy(off).wait_recv()

        r = rowpiece(b, block)
        full = lax.dot_general(X[r, :], E[...], NT, preferred_element_type=F32) + corr_row
        pick(r, full)
        return carry

    lax.fori_loop(0, n // 2, encode, 0)

    def reduce_own(phase, after_first, after_third):
        peer_c, peer_y = z * 4 + y * 2 + (1 - c), z * 4 + (1 - y) * 2 + c
        half, quarter = 2 * nz * rows, nz * rows
        one = remote(PP.at[rowpiece(1 - c, half)], R1.at[phase], ar_send.at[phase, 0], ar_recv.at[phase, 0], peer_c)
        one.start()
        after_first()
        one.wait()
        mine_half = c * 2

        def add(base_rows, buffer, pieces):
            def go(i, carry):
                r = rowpiece(base_rows + i)
                PP[r, :] = PP[r, :] + buffer[phase, rowpiece(i), :]
                return carry

            lax.fori_loop(0, pieces, go, 0)

        add(c * 2 * nz, R1, 2 * nz)
        two = remote(PP.at[rowpiece(mine_half + 1 - y, quarter)], R2.at[phase], ar_send.at[phase, 1], ar_recv.at[phase, 1], peer_y)
        two.start()
        two.wait()
        add((mine_half + y) * nz, R2, nz)
        third = []
        for dz in range(1, nz):
            oz = (z + dz) % nz
            copy = remote(PP.at[rowpiece((mine_half + y) * nz + oz)], R3.at[phase, dz - 1],
                          ar_send.at[phase, 1 + dz], ar_recv.at[phase, 1 + dz], oz * 4 + y * 2 + c)
            copy.start()
            third.append(copy)
        after_third()
        for copy in third:
            copy.wait()
        total = PP[rowpiece(mine), :]
        for dz in range(1, nz):
            total = total + R3[phase, dz - 1]
        return total

    def spread(phase, between=lambda: None):
        peer_c, peer_y = z * 4 + y * 2 + (1 - c), z * 4 + (1 - y) * 2 + c
        half, quarter = 2 * nz * rows, nz * rows
        base = 1 + nz
        piece = ACT.at[phase, rowpiece(mine)]
        copies = []
        for dz in range(1, nz):
            oz = (z + dz) % nz
            copy = remote(piece, piece, ar_send.at[phase, base + dz], ar_recv.at[phase, base + dz], oz * 4 + y * 2 + c)
            copy.start()
            copies.append(copy)
        between()
        for copy in copies:
            copy.wait()
        piece = ACT.at[phase, rowpiece(c * 2 + y, quarter)]
        copy = remote(piece, piece, ar_send.at[phase, base + nz], ar_recv.at[phase, base + nz], peer_y)
        copy.start()
        copy.wait()
        piece = ACT.at[phase, rowpiece(c, half)]
        copy = remote(piece, piece, ar_send.at[phase, base + nz + 1], ar_recv.at[phase, base + nz + 1], peer_c)
        copy.start()
        copy.wait()

    pre = reduce_own(0, lambda: None, lambda: each(pass_on(fcopy, fcross)))
    PRE[...] = pre
    ACT[0, rowpiece(mine), :] = (pre / (1.0 + jnp.exp(-pre))).astype(BF)
    spread(0)

    each(lambda off: fcopy(off).wait_send())
    each(lambda off: fcross(off).wait())

    def outbound(kind, src, dst):
        def make(off):
            place, dev = far(off)
            return remote(src.at[rowpiece(place)], dst.at[:, colpiece(mine)],
                          send.at[kind, off], recv.at[kind, off], dev)

        return make

    def keep(src, dst, slot):
        return pltpu.make_async_copy(src.at[rowpiece(mine)], dst.at[:, colpiece(mine)], local.at[slot])

    rcopy = outbound(SR, RO, recon_out)
    dcopy = outbound(SGD, GD, gdec_out)
    gcopy = outbound(SGE, GE, genc_out)
    keeps = [keep(RO, recon_out, 4), keep(GD, gdec_out, 5), keep(GE, genc_out, 6)]

    def decode(i, carry):
        b = (mine // 2 + i) % (n // 2)
        r = rowpiece(b, block)
        act = ACT[0, r, :]
        t0, t1 = TC[r, 0:1], TC[r, 1:2]
        a0, a1 = act[:, :lat].astype(F32), act[:, lat:].astype(F32)
        wide = jnp.concatenate(
            [jnp.where(t0 == float(s), a0, jnp.where(t1 == float(s), a1, 0.0)).astype(BF) for s in range(n)],
            axis=1,
        )
        recon_f = jnp.dot(wide, F[...], preferred_element_type=F32) + db_row
        RO[r, :] = recon_f.astype(BF)
        for q in range(2):
            off = (2 * b + q - mine + n) % n

            @pl.when(off != 0)
            def _():
                rcopy(off).start()

        err = (recon_f - X[r, :].astype(F32)).astype(BF)
        ERR[r, :] = err
        pick(r, lax.dot_general(err, F[...], NT, preferred_element_type=F32))
        return carry

    lax.fori_loop(0, n // 2, decode, 0)

    def turn(phase):
        def go(p, carry):
            ACTT[:, lanepiece(p)] = jnp.transpose(ACT[phase, rowpiece(p), :].astype(F32)).astype(BF)
            return carry

        lax.fori_loop(0, n, go, 0)

    def grad_tile(s, other):
        sf = jnp.asarray(s, jnp.int32).astype(F32)
        t0, t1 = TR[0:1, :], TR[1:2, :]
        picked = jnp.where(
            t0 == sf,
            ACTT[:lat, :].astype(F32),
            jnp.where(t1 == sf, ACTT[lat:, :].astype(F32), 0.0),
        ).astype(BF)
        return jnp.dot(picked, other[...], preferred_element_type=F32)

    def decoder_grad():
        turn(0)

        def go(off):
            s = (mine + off) % n
            GD[rowpiece(s), :] = grad_tile(s, ERR).astype(BF)

        go(0)
        each(go)

    def first():
        keeps[0].start()
        decoder_grad()

    def third():
        each(lambda off: dcopy(off).start())
        keeps[1].start()

    slope = reduce_own(1, first, third)
    value = PRE[...]
    sig = 1.0 / (1.0 + jnp.exp(-value))
    dpre = slope * (sig * (1.0 + value * (1.0 - sig)))
    ACT[1, rowpiece(mine), :] = dpre.astype(BF)
    t0, t1 = TC[rowpiece(mine), 0:1], TC[rowpiece(mine), 1:2]
    for s in range(n):
        share = jnp.where(t0 == float(s), dpre[:, :lat], 0.0) + jnp.where(t1 == float(s), dpre[:, lat:], 0.0)
        GT[s : s + 1, :] = jnp.sum(share, axis=0, keepdims=True)

    def bcopy(off):
        place, dev = far(off)
        return remote(GT, GB.at[mine], send.at[SGB, off], recv.at[SGB, off], dev)

    each(lambda off: bcopy(off).start())
    spread(1)
    GB[mine] = GT[...]
    each(lambda off: bcopy(off).wait())
    grad_b = jnp.sum(GB[...], axis=0)
    grad_cols = jnp.transpose(grad_b)
    gb_out[...] = grad_b
    turn(1)

    def encoder_grad(off):
        s = (mine + off) % n
        lane = lax.broadcasted_iota(jnp.int32, (lat, n), 1)
        col = jnp.sum(jnp.where(lane == s, grad_cols, 0.0), axis=1, keepdims=True)
        GE[rowpiece(s), :] = (grad_tile(s, X) - col * db_row).astype(BF)

    def encoder_step(off):
        encoder_grad(off)
        gcopy(off).start()

    each(encoder_step)
    encoder_grad(0)
    keeps[2].start()
    each(lambda off: rcopy(off).wait())
    each(lambda off: dcopy(off).wait())
    each(lambda off: gcopy(off).wait())
    for copy in keeps:
        copy.wait()


def sliced_body(acts, block_ids, slot_of, enc_tiles, dec_tiles, enc_bias, dec_bias):
    n = lax.axis_size("latent")
    nz = n // 4
    rows, width = acts.shape
    lat = enc_tiles.shape[1]
    cols = width // n
    me = lax.axis_index("latent")
    mine = place_of(me, nz)
    picked = block_ids[:, :, None] == jnp.arange(n, dtype=jnp.int32)[None, None, :]
    target = jnp.sum(jnp.where(picked, place_of(slot_of, nz)[None, None, :], 0), axis=2)
    tgt = jnp.zeros((8, rows), F32).at[:2].set(target.T.astype(F32))
    db = lax.dynamic_slice(dec_bias, (mine * cols,), (cols,)).astype(F32)
    db = jnp.broadcast_to(db[None, :], (8, cols))
    here = jnp.arange(n, dtype=jnp.int32) == mine
    bias = jnp.where(here[:, None], enc_bias[0][None, :], 0.0).reshape(1, n * lat)
    bias = jnp.broadcast_to(bias, (8, n * lat))
    hbm = pl.BlockSpec(memory_space=pl.ANY)
    vmem = pl.BlockSpec(memory_space=pltpu.VMEM)
    all_rows = n * rows
    sem = pltpu.SemaphoreType.DMA
    recon, genc, gdec, gb = pl.pallas_call(
        functools.partial(step_kernel, n),
        out_shape=(
            jax.ShapeDtypeStruct((rows, width), BF),
            jax.ShapeDtypeStruct((lat, width), BF),
            jax.ShapeDtypeStruct((lat, width), BF),
            jax.ShapeDtypeStruct((n, lat), F32),
        ),
        in_specs=[hbm, hbm, hbm, vmem, vmem, vmem],
        out_specs=(hbm, hbm, hbm, vmem),
        scratch_shapes=[
            pltpu.VMEM((all_rows, cols), BF),
            pltpu.VMEM((n * lat, cols), BF),
            pltpu.VMEM((n * lat, cols), BF),
            pltpu.VMEM((8, all_rows), F32),
            pltpu.VMEM((all_rows, 8), F32),
            pltpu.VMEM((all_rows, 2 * lat), F32),
            pltpu.VMEM((2, all_rows // 2, 2 * lat), F32),
            pltpu.VMEM((2, all_rows // 4, 2 * lat), F32),
            pltpu.VMEM((2, nz - 1, rows, 2 * lat), F32),
            pltpu.VMEM((2, all_rows, 2 * lat), BF),
            pltpu.VMEM((2 * lat, all_rows), BF),
            pltpu.VMEM((all_rows, cols), BF),
            pltpu.VMEM((all_rows, cols), BF),
            pltpu.VMEM((n * lat, cols), BF),
            pltpu.VMEM((n * lat, cols), BF),
            pltpu.VMEM((rows, 2 * lat), F32),
            pltpu.VMEM((n, n, lat), F32),
            pltpu.VMEM((n, lat), F32),
            sem((10, n)),
            sem((10, n)),
            sem((2, 4 + 2 * nz)),
            sem((2, 4 + 2 * nz)),
            sem((8,)),
        ],
        compiler_params=pltpu.CompilerParams(
            collective_id=0, has_side_effects=True, vmem_limit_bytes=56 * 1024 * 1024
        ),
        cost_estimate=pl.CostEstimate(
            flops=5 * 2 * all_rows * n * lat * cols, bytes_accessed=24 << 20, transcendentals=0
        ),
    )(acts, enc_tiles[0], dec_tiles[0], tgt, db, bias)
    bias_grad = jnp.sum(jnp.where(here[:, None], gb, 0.0), axis=0)
    return (recon, genc[None], gdec[None], bias_grad[None])


def silu_slope(value):
    sig = jax.nn.sigmoid(value)
    return sig * (1.0 + value * (1.0 - sig))


def encode_rows(rows, tile_enc, tile_dec, bias_row, dec_bias):
    pre = jnp.dot(rows, tile_enc.T, preferred_element_type=jnp.float32)
    pre = (
        pre
        - jnp.dot(dec_bias, tile_enc.T, preferred_element_type=jnp.float32)[None, :]
        + bias_row[None, :]
    )
    act = jax.nn.silu(pre).astype(jnp.bfloat16)
    part = jnp.dot(act, tile_dec, preferred_element_type=jnp.float32).astype(jnp.bfloat16)
    return (pre, act, part)


def routed_body(acts, block_ids, slot_of, enc_tiles, dec_tiles, enc_bias, dec_bias):
    devices = lax.axis_size("latent")
    tok_rows, topb = block_ids.shape
    width = acts.shape[1]
    nblk = slot_of.shape[0]
    capacity = 2 * tok_rows * topb // devices
    flat = block_ids.reshape(-1)
    pairs = flat.shape[0]
    picked = flat[:, None] == jnp.arange(nblk, dtype=jnp.int32)[None, :]
    target = jnp.sum(jnp.where(picked, slot_of[None, :], 0), axis=1)
    marks = (target[:, None] == jnp.arange(devices, dtype=jnp.int32)[None, :]).astype(jnp.int32)
    rank = jnp.sum((jnp.cumsum(marks, axis=0) - 1) * marks, axis=1)
    position = target * capacity + rank
    source = jnp.arange(pairs, dtype=jnp.int32) // topb
    outgoing = jnp.zeros((devices * capacity, width), jnp.bfloat16).at[position].set(acts[source])
    outgoing = outgoing.reshape(devices, capacity, width)
    tile_enc = enc_tiles[0]
    tile_dec = dec_tiles[0]
    bias_row = enc_bias[0]
    arrived = lax.all_to_all(outgoing, "latent", split_axis=0, concat_axis=0, tiled=True).reshape(
        devices * capacity, width
    )
    pre, act, part = encode_rows(arrived, tile_enc, tile_dec, bias_row, dec_bias)
    returned = lax.all_to_all(
        part.reshape(devices, capacity, width), "latent", split_axis=0, concat_axis=0, tiled=True
    )
    returned = returned.reshape(devices * capacity, width)
    gathered = returned[position].astype(jnp.float32).reshape(tok_rows, topb, width)
    recon_f = jnp.sum(gathered, axis=1) + dec_bias.astype(jnp.float32)[None, :]
    recon = recon_f.astype(jnp.bfloat16)
    err = (recon_f - acts.astype(jnp.float32)).astype(jnp.bfloat16)
    err_out = jnp.zeros((devices * capacity, width), jnp.bfloat16).at[position].set(err[source])
    errors = lax.all_to_all(
        err_out.reshape(devices, capacity, width), "latent", split_axis=0, concat_axis=0, tiled=True
    )
    errors = errors.reshape(devices * capacity, width)
    slope = jnp.dot(errors, tile_dec.T, preferred_element_type=jnp.float32) * silu_slope(pre)
    slope_b = slope.astype(jnp.bfloat16)
    bias_grad = jnp.sum(slope, axis=0)
    dec_grad = jnp.dot(act.T, errors, preferred_element_type=jnp.float32).astype(jnp.bfloat16)
    enc_grad = jnp.dot(slope_b.T, arrived, preferred_element_type=jnp.float32)
    enc_grad = (enc_grad - bias_grad[:, None] * dec_bias.astype(jnp.float32)[None, :]).astype(
        jnp.bfloat16
    )
    return (recon, enc_grad[None], dec_grad[None], bias_grad[None])


def body(acts, block_ids, slot_of, enc_tiles, dec_tiles, enc_bias, dec_bias):
    devices = lax.axis_size("latent")
    small = lax.axis_size("groups") == 2 and devices == 16 and block_ids.shape[1] == 2 and slot_of.shape[0] == devices
    chosen = sliced_body if small else routed_body
    return chosen(acts, block_ids, slot_of, enc_tiles, dec_tiles, enc_bias, dec_bias)


def solution(mesh):
    in_specs = (
        P(("groups", "latent"), None),
        P(("groups", "latent"), None),
        P(),
        P("latent", None, None),
        P("latent", None, None),
        P("latent", None),
        P(),
    )
    out_specs = (
        P(("groups", "latent"), None),
        P(("groups", "latent"), None, None),
        P(("groups", "latent"), None, None),
        P(("groups", "latent"), None),
    )
    return jax.shard_map(body, mesh=mesh, in_specs=in_specs, out_specs=out_specs, check_vma=False)
```

```python
import functools

import jax
import jax.numpy as jnp
from jax import lax
from jax.experimental import pallas as pl
from jax.experimental.pallas import tpu as pltpu
from jax.sharding import PartitionSpec as P

BF = jnp.bfloat16
F32 = jnp.float32
NT = (((1,), (1,)), ((), ()))
MESH = pl.DeviceIdType.MESH
SX, SE, SF, ST, SR, SGD, SGE, SGB, SEX, SFX = range(10)


def place_of(index, nz):
    return (index % 2) * (2 * nz) + ((index // 2) % 2) * nz + index // 4


def device_of(place, nz):
    return (place % nz) * 4 + ((place // nz) % 2) * 2 + place // (2 * nz)


def step_kernel(
    n,
    acts,
    enc,
    dec,
    ids_ref,
    slot_ref,
    db_ref,
    bias_ref,
    recon_out,
    genc_out,
    gdec_out,
    gb_out,
    X,
    E,
    F,
    TR,
    TC,
    PP,
    R1,
    R2,
    R3,
    ACT,
    ACTT,
    ERR,
    RO,
    GD,
    GE,
    PRE,
    GB,
    GT,
    tgt,
    send,
    recv,
    ar_send,
    ar_recv,
    local,
):
    nz = n // 4
    rows = acts.shape[0]
    cols = acts.shape[1] // n
    lat = enc.shape[0]
    me = lax.axis_index("latent")
    c = me % 2
    y = (me // 2) % 2
    z = me // 4
    mine = place_of(me, nz)
    g = lax.axis_index("groups")
    share = lat // 2

    def far(off):
        place = (mine + off) % n
        return place, device_of(place, nz)

    def remote(src, dst, ssem, rsem, dev):
        return pltpu.make_async_remote_copy(
            src_ref=src, dst_ref=dst, send_sem=ssem, recv_sem=rsem,
            device_id={"latent": dev}, device_id_type=MESH,
        )

    def colpiece(place):
        return pl.ds(pl.multiple_of(place * cols, cols), cols)

    def rowpiece(place, size=rows):
        return pl.ds(pl.multiple_of(place * size, size), size)

    def lanepiece(place):
        return pl.ds(pl.multiple_of(place * rows, rows), rows)

    def each(fn):
        def go(off, carry):
            fn(off)
            return carry

        lax.fori_loop(1, n, go, 0)

    barrier = pltpu.get_barrier_semaphore()

    def greet(off):
        pl.semaphore_signal(barrier, inc=1, device_id={"latent": far(off)[1]}, device_id_type=MESH)

    each(greet)
    twin = {"groups": 1 - g, "latent": me}
    pl.semaphore_signal(barrier, inc=1, device_id=twin, device_id_type=MESH)
    pl.semaphore_wait(barrier, n)

    def inbound(kind, src, dst):
        def make(off):
            place, dev = far(off)
            return remote(src.at[:, colpiece(place)], dst.at[rowpiece(mine)],
                          send.at[kind, off], recv.at[kind, off], dev)

        return make

    def tile_rows(place):
        return pl.ds(pl.multiple_of(place * lat + g * share, share), share)

    def tile_inbound(kind, src, dst):
        def make(off):
            place, dev = far(off)
            return remote(src.at[pl.ds(pl.multiple_of(g * share, share), share), colpiece(place)],
                          dst.at[tile_rows(mine)], send.at[kind, off], recv.at[kind, off], dev)

        return make

    def tile_forward(kind, dst):
        def make(off):
            piece = dst.at[tile_rows((mine - off + n) % n)]
            return pltpu.make_async_remote_copy(
                src_ref=piece, dst_ref=piece, send_sem=send.at[kind, off], recv_sem=recv.at[kind, off],
                device_id=twin, device_id_type=MESH,
            )

        return make

    def tcopy(off):
        place, dev = far(off)
        return remote(tgt, TR.at[:, lanepiece(mine)], send.at[ST, off], recv.at[ST, off], dev)

    xcopy = inbound(SX, acts, X)
    ecopy = tile_inbound(SE, enc, E)
    fcopy = tile_inbound(SF, dec, F)
    ecross = tile_forward(SEX, E)
    fcross = tile_forward(SFX, F)
    each(lambda off: ecopy(off).start())
    ids = ids_ref[...]
    named = jnp.zeros(ids.shape, F32)
    for b in range(n):
        named = jnp.where(ids == b, place_of(slot_ref[b], nz).astype(F32), named)
    tgt[...] = named
    each(lambda off: tcopy(off).start())
    each(lambda off: xcopy(off).start())
    own = [
        pltpu.make_async_copy(acts.at[:, colpiece(mine)], X.at[rowpiece(mine)], local.at[0]),
        pltpu.make_async_copy(enc.at[:, colpiece(mine)], E.at[rowpiece(mine)], local.at[1]),
        pltpu.make_async_copy(dec.at[:, colpiece(mine)], F.at[rowpiece(mine)], local.at[2]),
        pltpu.make_async_copy(tgt, TR.at[:, lanepiece(mine)], local.at[3]),
    ]
    for copy in own:
        copy.start()
    for copy in own:
        copy.wait()
    each(lambda off: tcopy(off).wait())

    def pass_on(copy, cross):
        def go(off):
            copy(off).wait_recv()
            cross(off).start()

        return go

    def columns(p, carry):
        TC[rowpiece(p), :] = jnp.transpose(TR[:, lanepiece(p)])
        return carry

    lax.fori_loop(0, n, columns, 0)
    each(pass_on(ecopy, ecross))
    each(lambda off: ecross(off).wait())

    db_row = db_ref[:, colpiece(mine)].astype(F32)
    db = jnp.broadcast_to(db_row, (16, cols)).astype(BF)
    lane_block = lax.broadcasted_iota(jnp.int32, (1, n * lat), 1) // lat
    bias = jnp.where(lane_block == mine, jnp.concatenate([bias_ref[...]] * n, axis=1), 0.0)
    corr = bias - lax.dot_general(db, E[...], NT, preferred_element_type=F32)
    corr_row = corr[0:1, :]
    block = 2 * rows

    def pick(r, full):
        for j in range(2):
            t = TC[r, j : j + 1]
            total = jnp.zeros((block, lat), F32)
            for s in range(n):
                total = jnp.where(t == float(s), full[:, s * lat : (s + 1) * lat], total)
            PP[r, j * lat : (j + 1) * lat] = total

    def encode(i, carry):
        b = (mine // 2 - i + n) % (n // 2)

        @pl.when(i == n // 2 - 2)
        def _():
            each(lambda off: ecopy(off).wait_send())
            each(lambda off: xcopy(off).wait_send())
            each(lambda off: fcopy(off).start())

        for q in range(2):
            off = (mine - 2 * b - q + n) % n

            @pl.when(off != 0)
            def _():
                xcopy(off).wait_recv()

        r = rowpiece(b, block)
        full = lax.dot_general(X[r, :], E[...], NT, preferred_element_type=F32) + corr_row
        pick(r, full)
        return carry

    lax.fori_loop(0, n // 2, encode, 0)

    def reduce_own(phase, after_first, after_third):
        peer_c, peer_y = z * 4 + y * 2 + (1 - c), z * 4 + (1 - y) * 2 + c
        half, quarter = 2 * nz * rows, nz * rows
        one = remote(PP.at[rowpiece(1 - c, half)], R1.at[phase], ar_send.at[phase, 0], ar_recv.at[phase, 0], peer_c)
        one.start()
        after_first()
        one.wait()
        mine_half = c * 2

        def add(base_rows, buffer, pieces):
            def go(i, carry):
                r = rowpiece(base_rows + i)
                PP[r, :] = PP[r, :] + buffer[phase, rowpiece(i), :]
                return carry

            lax.fori_loop(0, pieces, go, 0)

        add(c * 2 * nz, R1, 2 * nz)
        two = remote(PP.at[rowpiece(mine_half + 1 - y, quarter)], R2.at[phase], ar_send.at[phase, 1], ar_recv.at[phase, 1], peer_y)
        two.start()
        two.wait()
        add((mine_half + y) * nz, R2, nz)
        third = []
        for dz in range(1, nz):
            oz = (z + dz) % nz
            copy = remote(PP.at[rowpiece((mine_half + y) * nz + oz)], R3.at[phase, dz - 1],
                          ar_send.at[phase, 1 + dz], ar_recv.at[phase, 1 + dz], oz * 4 + y * 2 + c)
            copy.start()
            third.append(copy)
        after_third()
        for copy in third:
            copy.wait()
        total = PP[rowpiece(mine), :]
        for dz in range(1, nz):
            total = total + R3[phase, dz - 1]
        return total

    def spread(phase, between=lambda: None):
        peer_c, peer_y = z * 4 + y * 2 + (1 - c), z * 4 + (1 - y) * 2 + c
        half, quarter = 2 * nz * rows, nz * rows
        base = 1 + nz
        piece = ACT.at[phase, rowpiece(mine)]
        copies = []
        for dz in range(1, nz):
            oz = (z + dz) % nz
            copy = remote(piece, piece, ar_send.at[phase, base + dz], ar_recv.at[phase, base + dz], oz * 4 + y * 2 + c)
            copy.start()
            copies.append(copy)
        between()
        for copy in copies:
            copy.wait()
        piece = ACT.at[phase, rowpiece(c * 2 + y, quarter)]
        copy = remote(piece, piece, ar_send.at[phase, base + nz], ar_recv.at[phase, base + nz], peer_y)
        copy.start()
        copy.wait()
        piece = ACT.at[phase, rowpiece(c, half)]
        copy = remote(piece, piece, ar_send.at[phase, base + nz + 1], ar_recv.at[phase, base + nz + 1], peer_c)
        copy.start()
        copy.wait()

    pre = reduce_own(0, lambda: None, lambda: each(pass_on(fcopy, fcross)))
    PRE[...] = pre
    ACT[0, rowpiece(mine), :] = (pre / (1.0 + jnp.exp(-pre))).astype(BF)
    spread(0)

    each(lambda off: fcopy(off).wait_send())
    each(lambda off: fcross(off).wait())

    def outbound(kind, src, dst):
        def make(off):
            place, dev = far(off)
            return remote(src.at[rowpiece(place)], dst.at[:, colpiece(mine)],
                          send.at[kind, off], recv.at[kind, off], dev)

        return make

    def keep(src, dst, slot):
        return pltpu.make_async_copy(src.at[rowpiece(mine)], dst.at[:, colpiece(mine)], local.at[slot])

    rcopy = outbound(SR, RO, recon_out)
    dcopy = outbound(SGD, GD, gdec_out)
    gcopy = outbound(SGE, GE, genc_out)
    keeps = [keep(RO, recon_out, 4), keep(GD, gdec_out, 5), keep(GE, genc_out, 6)]

    def decode(i, carry):
        b = (mine // 2 + i) % (n // 2)
        r = rowpiece(b, block)
        act = ACT[0, r, :]
        t0, t1 = TC[r, 0:1], TC[r, 1:2]
        a0, a1 = act[:, :lat].astype(F32), act[:, lat:].astype(F32)
        wide = jnp.concatenate(
            [jnp.where(t0 == float(s), a0, jnp.where(t1 == float(s), a1, 0.0)).astype(BF) for s in range(n)],
            axis=1,
        )
        recon_f = jnp.dot(wide, F[...], preferred_element_type=F32) + db_row
        RO[r, :] = recon_f.astype(BF)
        for q in range(2):
            off = (2 * b + q - mine + n) % n

            @pl.when(off != 0)
            def _():
                rcopy(off).start()

        err = (recon_f - X[r, :].astype(F32)).astype(BF)
        ERR[r, :] = err
        pick(r, lax.dot_general(err, F[...], NT, preferred_element_type=F32))
        return carry

    lax.fori_loop(0, n // 2, decode, 0)

    def turn(phase):
        def go(p, carry):
            ACTT[:, lanepiece(p)] = jnp.transpose(ACT[phase, rowpiece(p), :].astype(F32)).astype(BF)
            return carry

        lax.fori_loop(0, n, go, 0)

    def grad_tile(s, other):
        sf = jnp.asarray(s, jnp.int32).astype(F32)
        t0, t1 = TR[0:1, :], TR[1:2, :]
        picked = jnp.where(
            t0 == sf,
            ACTT[:lat, :].astype(F32),
            jnp.where(t1 == sf, ACTT[lat:, :].astype(F32), 0.0),
        ).astype(BF)
        return jnp.dot(picked, other[...], preferred_element_type=F32)

    def decoder_grad():
        turn(0)

        def go(off):
            s = (mine + off) % n
            GD[rowpiece(s), :] = grad_tile(s, ERR).astype(BF)

        go(0)
        each(go)

    def first():
        keeps[0].start()
        decoder_grad()

    def third():
        each(lambda off: dcopy(off).start())
        keeps[1].start()

    slope = reduce_own(1, first, lambda: None)
    value = PRE[...]
    sig = 1.0 / (1.0 + jnp.exp(-value))
    dpre = slope * (sig * (1.0 + value * (1.0 - sig)))
    ACT[1, rowpiece(mine), :] = dpre.astype(BF)
    t0, t1 = TC[rowpiece(mine), 0:1], TC[rowpiece(mine), 1:2]
    for s in range(n):
        share = jnp.where(t0 == float(s), dpre[:, :lat], 0.0) + jnp.where(t1 == float(s), dpre[:, lat:], 0.0)
        GT[s : s + 1, :] = jnp.sum(share, axis=0, keepdims=True)

    def bcopy(off):
        place, dev = far(off)
        return remote(GT, GB.at[mine], send.at[SGB, off], recv.at[SGB, off], dev)

    each(lambda off: bcopy(off).start())
    spread(1, third)
    GB[mine] = GT[...]
    each(lambda off: bcopy(off).wait())
    grad_b = jnp.sum(GB[...], axis=0)
    grad_cols = jnp.transpose(grad_b)
    row = lax.broadcasted_iota(jnp.int32, (n, lat), 0)
    gb_out[...] = jnp.sum(jnp.where(row == mine, grad_b, 0.0), axis=0, keepdims=True)
    turn(1)

    def encoder_grad(off):
        s = (mine + off) % n
        lane = lax.broadcasted_iota(jnp.int32, (lat, n), 1)
        col = jnp.sum(jnp.where(lane == s, grad_cols, 0.0), axis=1, keepdims=True)
        GE[rowpiece(s), :] = (grad_tile(s, X) - col * db_row).astype(BF)

    def encoder_step(off):
        encoder_grad(off)
        gcopy(off).start()

    each(encoder_step)
    encoder_grad(0)
    keeps[2].start()
    each(lambda off: rcopy(off).wait())
    each(lambda off: dcopy(off).wait())
    each(lambda off: gcopy(off).wait())
    for copy in keeps:
        copy.wait()


def sliced_body(acts, block_ids, slot_of, enc_tiles, dec_tiles, enc_bias, dec_bias):
    n = lax.axis_size("latent")
    nz = n // 4
    rows, width = acts.shape
    lat = enc_tiles.shape[1]
    cols = width // n
    ids = jnp.pad(block_ids.T, ((0, 6), (0, 0)))
    hbm = pl.BlockSpec(memory_space=pl.ANY)
    vmem = pl.BlockSpec(memory_space=pltpu.VMEM)
    all_rows = n * rows
    sem = pltpu.SemaphoreType.DMA
    recon, genc, gdec, gb = pl.pallas_call(
        functools.partial(step_kernel, n),
        out_shape=(
            jax.ShapeDtypeStruct((rows, width), BF),
            jax.ShapeDtypeStruct((lat, width), BF),
            jax.ShapeDtypeStruct((lat, width), BF),
            jax.ShapeDtypeStruct((1, lat), F32),
        ),
        in_specs=[hbm, hbm, hbm, vmem, pl.BlockSpec(memory_space=pltpu.SMEM), vmem, vmem],
        out_specs=(hbm, hbm, hbm, vmem),
        scratch_shapes=[
            pltpu.VMEM((all_rows, cols), BF),
            pltpu.VMEM((n * lat, cols), BF),
            pltpu.VMEM((n * lat, cols), BF),
            pltpu.VMEM((8, all_rows), F32),
            pltpu.VMEM((all_rows, 8), F32),
            pltpu.VMEM((all_rows, 2 * lat), F32),
            pltpu.VMEM((2, all_rows // 2, 2 * lat), F32),
            pltpu.VMEM((2, all_rows // 4, 2 * lat), F32),
            pltpu.VMEM((2, nz - 1, rows, 2 * lat), F32),
            pltpu.VMEM((2, all_rows, 2 * lat), BF),
            pltpu.VMEM((2 * lat, all_rows), BF),
            pltpu.VMEM((all_rows, cols), BF),
            pltpu.VMEM((all_rows, cols), BF),
            pltpu.VMEM((n * lat, cols), BF),
            pltpu.VMEM((n * lat, cols), BF),
            pltpu.VMEM((rows, 2 * lat), F32),
            pltpu.VMEM((n, n, lat), F32),
            pltpu.VMEM((n, lat), F32),
            pltpu.VMEM((8, rows), F32),
            sem((10, n)),
            sem((10, n)),
            sem((2, 4 + 2 * nz)),
            sem((2, 4 + 2 * nz)),
            sem((8,)),
        ],
        compiler_params=pltpu.CompilerParams(
            collective_id=0, has_side_effects=True, vmem_limit_bytes=56 * 1024 * 1024
        ),
        cost_estimate=pl.CostEstimate(
            flops=5 * 2 * all_rows * n * lat * cols, bytes_accessed=24 << 20, transcendentals=0
        ),
    )(acts, enc_tiles[0], dec_tiles[0], ids, slot_of, dec_bias.reshape(1, width), enc_bias)
    return (recon, genc[None], gdec[None], gb)


def silu_slope(value):
    sig = jax.nn.sigmoid(value)
    return sig * (1.0 + value * (1.0 - sig))


def encode_rows(rows, tile_enc, tile_dec, bias_row, dec_bias):
    pre = jnp.dot(rows, tile_enc.T, preferred_element_type=jnp.float32)
    pre = (
        pre
        - jnp.dot(dec_bias, tile_enc.T, preferred_element_type=jnp.float32)[None, :]
        + bias_row[None, :]
    )
    act = jax.nn.silu(pre).astype(jnp.bfloat16)
    part = jnp.dot(act, tile_dec, preferred_element_type=jnp.float32).astype(jnp.bfloat16)
    return (pre, act, part)


def routed_body(acts, block_ids, slot_of, enc_tiles, dec_tiles, enc_bias, dec_bias):
    devices = lax.axis_size("latent")
    tok_rows, topb = block_ids.shape
    width = acts.shape[1]
    nblk = slot_of.shape[0]
    capacity = 2 * tok_rows * topb // devices
    flat = block_ids.reshape(-1)
    pairs = flat.shape[0]
    picked = flat[:, None] == jnp.arange(nblk, dtype=jnp.int32)[None, :]
    target = jnp.sum(jnp.where(picked, slot_of[None, :], 0), axis=1)
    marks = (target[:, None] == jnp.arange(devices, dtype=jnp.int32)[None, :]).astype(jnp.int32)
    rank = jnp.sum((jnp.cumsum(marks, axis=0) - 1) * marks, axis=1)
    position = target * capacity + rank
    source = jnp.arange(pairs, dtype=jnp.int32) // topb
    outgoing = jnp.zeros((devices * capacity, width), jnp.bfloat16).at[position].set(acts[source])
    outgoing = outgoing.reshape(devices, capacity, width)
    tile_enc = enc_tiles[0]
    tile_dec = dec_tiles[0]
    bias_row = enc_bias[0]
    arrived = lax.all_to_all(outgoing, "latent", split_axis=0, concat_axis=0, tiled=True).reshape(
        devices * capacity, width
    )
    pre, act, part = encode_rows(arrived, tile_enc, tile_dec, bias_row, dec_bias)
    returned = lax.all_to_all(
        part.reshape(devices, capacity, width), "latent", split_axis=0, concat_axis=0, tiled=True
    )
    returned = returned.reshape(devices * capacity, width)
    gathered = returned[position].astype(jnp.float32).reshape(tok_rows, topb, width)
    recon_f = jnp.sum(gathered, axis=1) + dec_bias.astype(jnp.float32)[None, :]
    recon = recon_f.astype(jnp.bfloat16)
    err = (recon_f - acts.astype(jnp.float32)).astype(jnp.bfloat16)
    err_out = jnp.zeros((devices * capacity, width), jnp.bfloat16).at[position].set(err[source])
    errors = lax.all_to_all(
        err_out.reshape(devices, capacity, width), "latent", split_axis=0, concat_axis=0, tiled=True
    )
    errors = errors.reshape(devices * capacity, width)
    slope = jnp.dot(errors, tile_dec.T, preferred_element_type=jnp.float32) * silu_slope(pre)
    slope_b = slope.astype(jnp.bfloat16)
    bias_grad = jnp.sum(slope, axis=0)
    dec_grad = jnp.dot(act.T, errors, preferred_element_type=jnp.float32).astype(jnp.bfloat16)
    enc_grad = jnp.dot(slope_b.T, arrived, preferred_element_type=jnp.float32)
    enc_grad = (enc_grad - bias_grad[:, None] * dec_bias.astype(jnp.float32)[None, :]).astype(
        jnp.bfloat16
    )
    return (recon, enc_grad[None], dec_grad[None], bias_grad[None])


def body(acts, block_ids, slot_of, enc_tiles, dec_tiles, enc_bias, dec_bias):
    devices = lax.axis_size("latent")
    small = lax.axis_size("groups") == 2 and devices == 16 and block_ids.shape[1] == 2 and slot_of.shape[0] == devices
    chosen = sliced_body if small else routed_body
    return chosen(acts, block_ids, slot_of, enc_tiles, dec_tiles, enc_bias, dec_bias)


def solution(mesh):
    in_specs = (
        P(("groups", "latent"), None),
        P(("groups", "latent"), None),
        P(),
        P("latent", None, None),
        P("latent", None, None),
        P("latent", None),
        P(),
    )
    out_specs = (
        P(("groups", "latent"), None),
        P(("groups", "latent"), None, None),
        P(("groups", "latent"), None, None),
        P(("groups", "latent"), None),
    )
    return jax.shard_map(body, mesh=mesh, in_specs=in_specs, out_specs=out_specs, check_vma=False)
```
